32 devices in a mesh: ctx: 8 (over y, x, core), head: 4 (over z).
Axes of the slice: x: 2, y: 2, z: 4, core: 2. Of those that a mesh axis runs over, the one named last changes fastest.
Arguments:
- activations: bfloat16 [4096, 4096], P('ctx')
- qkv_weight: bfloat16 [4096, 3, 32, 128], P(None, None, 'head'), may hold values from -0.09375 to 0.09375
- out_weight: bfloat16 [32, 128, 4096], P('head'), may hold values from -0.09375 to 0.09375
- mod_table: float32 [16, 4096], replicated, may hold values from -3 to 3
- clip_level: int32 [32], replicated, may hold values from 0 to 15
- clip_of: int32 [4096], P('ctx'), may hold values from 0 to 31, never falling along the last dimension, each value on 1 to 256 neighbouring positions
- visible: int32 [32, 32], replicated, may hold values from 0 to 1, as said below
Outputs:
- mixed: bfloat16 [4096, 4096], P(('ctx', 'head'))
The draws below stay inside these ranges and needn't reach their ends.
Inputs may be any that keep to these rules, and one draw needn't show every extreme that they name: visible is 1 on the diagonal and 0 above it. `clip_of`: clip numbers never fall along the tokens; every clip has 1 to 256 tokens and one has exactly 256.
All inputs are finite; a program needn't handle non-finite values.
Results may differ from the reference program's by a relative error of at most 0.02.
The reference program's roundings to bfloat16 on the way count: a program that leaves them out, or rounds other values in their place, can miss the bound.
Values may be sent and summed in bfloat16 or wider, within the bound.
A program may use at most 128 MiB of HBM per device.

```python
import math
import jax
import jax.numpy as jnp
import numpy as np
from jax import lax

D = 4096
HEADS = 32
HDIM = 128
TOKENS = 4096
CLIPS = 32
CLIP_MOST = 256
LEVELS = 16


def draw_activations(key, part):
    first_key = jax.random.fold_in(key, 0)
    values = jax.random.normal(first_key, (TOKENS, D), jnp.float32)
    return values.astype(jnp.bfloat16)


def draw_visible(key, part):
    draws = jax.random.randint(key, (CLIPS, CLIPS), 0, 4)
    row_ids = lax.broadcasted_iota(jnp.int32, (CLIPS, CLIPS), 0)
    col_ids = lax.broadcasted_iota(jnp.int32, (CLIPS, CLIPS), 1)
    below = jnp.where(draws > 0, 1, 0)
    return jnp.where(col_ids == row_ids, 1, jnp.where(col_ids < row_ids, below, 0)).astype(jnp.int32)


def place_ends(array, rng, least, largest):
    dims = array.shape
    index_at = [jax.random.randint(jax.random.fold_in(rng, axis), (), 0, dims[axis]) for axis in range(len(dims))]
    array = array.at[tuple(index_at)].set(least)
    longest = dims.index(max(dims))
    index_at[longest] = (index_at[longest] + 1) % dims[longest]
    return array.at[tuple(index_at)].set(largest)


def steps_of(key, dims, shards, least, top_value):
    level, own = 1.0, jax.random.fold_in(key, 6)
    for axis_at, parts in shards:
        heights = jnp.exp(jax.random.uniform(jax.random.fold_in(own, axis_at), (parts,), jnp.float32, least / len(shards), top_value / len(shards)))
        level = level * jnp.repeat(heights, dims[axis_at] // parts).reshape([-1 if axis == axis_at else 1 for axis in range(len(dims))])
    return level


def split_up(count, total, limit, skew):
    loads = [(1 << 20) // math.isqrt(standing ** skew) + 1 for standing in range(2, count + 1)]
    spare, counts = total - limit - (count - 1), [1] * (count - 1)
    while spare > 0:
        movable = [i for i in range(count - 1) if counts[i] < limit]
        whole, left = sum([loads[i] for i in movable]), spare
        for i in movable:
            extra = min(limit - counts[i], max(1, left * loads[i] // whole), spare)
            counts[i] = counts[i] + extra
            spare = spare - extra
    return np.array([limit] + counts)


def uneven_parts(stream_key, count, total, limit, lean):
    if count == 2:
        one = jax.random.randint(stream_key, (), max(1, total - limit), min(limit, total - 1) + 1)
        return jnp.stack([one, total - one])
    sizes = jnp.asarray(split_up(count, total, limit, lean), jnp.int32)
    pairs = (count - 1) // 2
    source_of, sink = sizes[1:1 + 2 * pairs:2], sizes[2:2 + 2 * pairs:2]
    room = jnp.minimum(source_of - 1, limit - sink)
    shifted = jax.random.randint(jax.random.fold_in(stream_key, 1), (pairs,), 0, 1 << 20) % (room + 1)
    sizes = sizes.at[1:1 + 2 * pairs:2].set(source_of - shifted).at[2:2 + 2 * pairs:2].set(sink + shifted)
    return sizes[jax.random.permutation(jax.random.fold_in(stream_key, 2), count)]


def noise(rng, extent, scale, reach, pieces=(), dtype=jnp.bfloat16):
    values = scale * jax.random.normal(rng, extent, jnp.float32)
    if pieces:
        values = values * steps_of(rng, extent, pieces, -0.22, 0.18)
    return jnp.clip(values, -reach, reach).astype(dtype)


def setup_inputs(seed: int = 0) -> dict:
    splits = jax.random.split(jax.random.key(seed), 8)
    return {
        "activations": draw_activations(jax.random.fold_in(splits[7], 71), 0),
        "qkv_weight": noise(splits[1], (D, 3, HEADS, HDIM), D ** -0.5, 0.09375, ((2, 4),)),
        "out_weight": noise(splits[2], (HEADS, HDIM, D), (HEADS * HDIM) ** -0.5, 0.09375, ((0, 4),)),
        "mod_table": noise(splits[3], (LEVELS, D), 0.4, 3.0, (), jnp.float32),
        "clip_level": place_ends(jax.random.randint(splits[4], (CLIPS,), 0, LEVELS), jax.random.fold_in(splits[4], 1), 0, LEVELS - 1).astype(jnp.int32),
        "clip_of": jnp.searchsorted(jnp.cumsum(uneven_parts(splits[5], CLIPS, TOKENS, CLIP_MOST, 2)), jnp.arange(TOKENS), side="right").astype(jnp.int32),
        "visible": draw_visible(jax.random.fold_in(splits[7], 71), 0),
    }


def reference(activations, qkv_weight, out_weight, mod_table, clip_level, clip_of, visible):
    level_tok = clip_level[clip_of]
    moduled = (activations.astype(jnp.float32) * (1.0 + mod_table[level_tok])).astype(jnp.bfloat16)
    qkv = jnp.einsum('td,dchk->tchk', moduled.astype(jnp.float32), qkv_weight.astype(jnp.float32)).astype(jnp.bfloat16)
    queries = qkv[:, 0]
    key_rows = qkv[:, 1]
    value_rows = qkv[:, 2]
    allowed = visible[clip_of][:, clip_of] > 0
    score_scale = 1.0 / jnp.sqrt(jnp.float32(HDIM))

    def single_head(head_index):
        q_head = queries[:, head_index]
        k_head = key_rows[:, head_index]
        v_head = value_rows[:, head_index]
        scores = jnp.dot(q_head, k_head.T, preferred_element_type=jnp.float32) * score_scale
        masked = jnp.where(allowed, scores, -jnp.inf)
        top_score = lax.optimization_barrier(jnp.max(masked, axis=1, keepdims=True))
        weights = jnp.where(allowed, jnp.exp(scores - top_score), 0.0)
        totals = lax.optimization_barrier(jnp.sum(weights, axis=1, keepdims=True))
        summed = jnp.dot(weights.astype(jnp.bfloat16), v_head, preferred_element_type=jnp.float32)
        return (summed / totals).astype(jnp.bfloat16)
    attended = lax.map(single_head, jnp.arange(HEADS))
    mixed = jnp.einsum('htd,hdo->to', attended.astype(jnp.float32), out_weight.astype(jnp.float32))
    return mixed.astype(jnp.bfloat16)
```

```python
import functools
import math

import jax
import jax.numpy as jnp
from jax import lax
from jax.experimental import pallas as pl
from jax.experimental.pallas import tpu as pltpu
from jax.sharding import PartitionSpec as P


def score_block(state_now, kv_block, key_clips, queries, query_vis, score_scale):
    clip_count = query_vis.shape[1]
    clip_ids = lax.broadcasted_iota(jnp.int32, (1, clip_count), 1)
    key_hot = (key_clips[:, None] == clip_ids).astype(jnp.float32)
    allowed = jnp.dot(query_vis, key_hot.T, precision=lax.Precision.HIGHEST) > 0.5
    top_score, totals, summed = state_now
    key_rows = kv_block[:, 0]
    value_rows = kv_block[:, 1]
    scores = (
        jnp.einsum("rhd,khd->hrk", queries, key_rows, preferred_element_type=jnp.float32)
        * score_scale
    )
    masked = jnp.where(allowed[None], scores, -1e30)
    new_top = jnp.maximum(top_score, jnp.max(masked, axis=2))
    weights = jnp.where(allowed[None], jnp.exp(masked - new_top[:, :, None]), 0.0)
    factor = jnp.exp(top_score - new_top)
    totals = totals * factor + jnp.sum(weights, axis=2)
    summed = summed * factor[:, :, None] + jnp.einsum(
        "hrk,khd->hrd", weights.astype(jnp.bfloat16), value_rows, preferred_element_type=jnp.float32
    )
    return (new_top, totals, summed)


def fold_keys(state_now, kv_rows, key_clips, queries, query_vis, score_scale):
    key_count = kv_rows.shape[0]
    block_rows = math.gcd(key_count, 512)

    def one_block(block_index, state_in):
        first_row = block_index * block_rows
        kv_block = lax.dynamic_slice_in_dim(kv_rows, first_row, block_rows, 0)
        clip_block = lax.dynamic_slice_in_dim(key_clips, first_row, block_rows, 0)
        return score_block(state_in, kv_block, clip_block, queries, query_vis, score_scale)

    return lax.fori_loop(0, key_count // block_rows, one_block, state_now)


def per_device(activations, qkv_weight, out_weight, mod_table, clip_level, clip_of, visible):
    heads_here = qkv_weight.shape[2]
    head_size = qkv_weight.shape[3]
    clip_count = visible.shape[0]
    level_count = mod_table.shape[0]
    clip_ids = lax.broadcasted_iota(jnp.int32, (1, clip_count), 1)
    level_ids = lax.broadcasted_iota(jnp.int32, (1, level_count), 1)
    tok_hot = clip_of[:, None] == clip_ids
    level_rows = jnp.sum(jnp.where(tok_hot, clip_level[None, :], 0), axis=1)
    level_hot = (level_rows[:, None] == level_ids).astype(jnp.float32)
    modulation = jnp.dot(level_hot, mod_table, precision=lax.Precision.HIGHEST)
    moduled = (activations.astype(jnp.float32) * (1.0 + modulation)).astype(jnp.bfloat16)
    qkv = jnp.einsum(
        "td,dchk->tchk", moduled, qkv_weight, preferred_element_type=jnp.float32
    ).astype(jnp.bfloat16)
    queries = qkv[:, 0]
    kv_local = qkv[:, 1:3]
    query_count = queries.shape[0]
    query_hot = (clip_of[:, None] == clip_ids).astype(jnp.float32)
    query_vis = jnp.dot(query_hot, visible.astype(jnp.float32), precision=lax.Precision.HIGHEST)
    score_scale = 1.0 / jnp.sqrt(jnp.float32(head_size))
    initial = (
        jnp.full((heads_here, query_count), -1e30, jnp.float32),
        jnp.zeros((heads_here, query_count), jnp.float32),
        jnp.zeros((heads_here, query_count, head_size), jnp.float32),
    )
    kv_all, clips_all = (
        lax.all_gather(kv_local, "ctx", axis=0, tiled=True),
        lax.all_gather(clip_of, "ctx", axis=0, tiled=True),
    )
    final = fold_keys(initial, kv_all, clips_all, queries, query_vis, score_scale)
    attended = (final[2] / final[1][:, :, None]).astype(jnp.bfloat16)
    attended_rows = jnp.transpose(attended, (1, 0, 2))
    return lax.psum_scatter(
        jnp.einsum(
            "rhd,hdo->ro", attended_rows, out_weight, preferred_element_type=jnp.float32
        ).astype(jnp.bfloat16),
        "head",
        scatter_dimension=0,
        tiled=True,
    )


def exchange(sources, targets, sends, recvs, peer):
    return [
        pltpu.make_async_remote_copy(
            src_ref=source,
            dst_ref=target,
            send_sem=send,
            recv_sem=recv,
            device_id={"ctx": peer},
            device_id_type=pl.DeviceIdType.MESH,
        )
        for source, target, send, recv in zip(sources, targets, sends, recvs)
    ]


def attend_kernel(
    n, score_scale, qkv_ref, clip_ref, bias_ref, out_ref,
    query_buf, key_buf, value_buf, clip_buf, score_buf, top_buf, sum_buf, done_buf,
    send_sem, recv_sem, local_sem, back_send, back_recv, back_local,
):
    me = lax.axis_index("ctx")
    rows = qkv_ref.shape[2]
    size = qkv_ref.shape[3]
    lanes = clip_ref.shape[1]

    def span(block):
        return pl.ds(pl.multiple_of(block * rows, rows), rows)

    def landing(owner):
        return [
            query_buf.at[span(owner), pl.ds(0, size)],
            key_buf.at[span(owner), pl.ds(0, size)],
            value_buf.at[span(owner), pl.ds(0, size)],
            clip_buf.at[owner],
        ]

    def leaving(peer):
        return [qkv_ref.at[0, peer], qkv_ref.at[1, peer], qkv_ref.at[2, peer], clip_ref]

    barrier = pltpu.get_barrier_semaphore()
    for step in range(1, n):
        pl.semaphore_signal(
            barrier, inc=1, device_id={"ctx": lax.rem(me + step, n)},
            device_id_type=pl.DeviceIdType.MESH,
        )
    pl.semaphore_wait(barrier, n - 1)

    def outgoing(peer):
        return exchange(
            leaving(peer), landing(me),
            [send_sem.at[item, peer] for item in range(4)],
            [recv_sem.at[item, me] for item in range(4)], peer,
        )

    def incoming(owner):
        return exchange(
            leaving(owner), landing(owner),
            [send_sem.at[item, owner] for item in range(4)],
            [recv_sem.at[item, owner] for item in range(4)], owner,
        )

    def send_step(step, carry):
        for copy in outgoing(lax.rem(me + step, n)):
            copy.start()
        return carry

    lax.fori_loop(1, n, send_step, 0)
    own = [
        pltpu.make_async_copy(source, target, local_sem.at[item])
        for item, (source, target) in enumerate(zip(leaving(me), landing(me)))
    ]
    for copy in own:
        copy.start()
    value_buf[:, size:] = jnp.ones((n * rows, size), value_buf.dtype)
    for copy in own:
        copy.wait()

    def take(owner):
        @pl.when(owner != me)
        def _():
            for copy in incoming(owner):
                copy.wait_recv()

        ids = lax.broadcasted_iota(jnp.int32, (lanes, lanes), 0)
        for part in range(rows // lanes):
            row = clip_buf[owner, pl.ds(part, 1), :]
            hot = jnp.where(ids == row, 1.0, 0.0).T.astype(jnp.bfloat16)
            at = pl.ds(pl.multiple_of(owner * rows + part * lanes, lanes), lanes)
            key_buf[at, size:] = hot
            query_buf[at, size:] = jnp.dot(
                hot, bias_ref[...], preferred_element_type=jnp.float32
            ).astype(jnp.bfloat16)

    def back(block):
        return exchange(
            [done_buf.at[block]], [out_ref.at[me]],
            [back_send.at[block]], [back_recv.at[me]], block,
        )[0]

    def back_in(owner):
        return exchange(
            [done_buf.at[owner]], [out_ref.at[owner]],
            [back_send.at[owner]], [back_recv.at[owner]], owner,
        )[0]

    own_back = pltpu.make_async_copy(done_buf.at[me], out_ref.at[me], back_local)
    take(0)

    def one_block(block, carry):
        @pl.when(block < n - 1)
        def _():
            take(block + 1)

        count = jnp.minimum(block + 2, n)
        top_buf[...] = jnp.full(top_buf.shape, -jnp.inf, jnp.float32)

        def score(at, inner):
            found = lax.dot_general(
                query_buf[span(block), :], key_buf[span(at), :],
                (((1,), (1,)), ((), ())), preferred_element_type=jnp.float32,
            )
            score_buf[at] = found
            top = top_buf[...]
            for part in range(rows // lanes):
                top = jnp.maximum(top, found[:, part * lanes : (part + 1) * lanes])
            top_buf[...] = top
            return inner

        lax.fori_loop(0, count, score, 0)
        highest = jnp.max(top_buf[...], axis=1, keepdims=True) * score_scale
        top_buf[...] = jnp.broadcast_to(highest, top_buf.shape)
        sum_buf[...] = jnp.zeros(sum_buf.shape, jnp.float32)

        def weigh(at, inner):
            top = top_buf[...]
            weights = jnp.concatenate(
                [
                    jnp.exp2(
                        score_buf[at, :, part * lanes : (part + 1) * lanes] * score_scale - top
                    ).astype(jnp.bfloat16)
                    for part in range(rows // lanes)
                ],
                axis=1,
            )
            sum_buf[...] += jnp.dot(
                weights, value_buf[span(at), :], preferred_element_type=jnp.float32
            )
            return inner

        lax.fori_loop(0, count, weigh, 0)
        done_buf[block] = (sum_buf[:, :size] / sum_buf[:, size:]).astype(jnp.bfloat16)

        @pl.when(block != me)
        def _():
            back(block).start()

        @pl.when(block == me)
        def _():
            own_back.start()

        return carry

    lax.fori_loop(0, n, one_block, 0)

    def finish(step, carry):
        peer = lax.rem(me + step, n)
        for copy in outgoing(peer):
            copy.wait_send()
        back(peer).wait_send()
        back_in(peer).wait_recv()
        return carry

    lax.fori_loop(1, n, finish, 0)
    own_back.wait()


def attend_heads(qkv, clip_rows, bias, n):
    _, heads, rows, size = qkv.shape
    lanes = clip_rows.shape[1]
    bf16, f32 = jnp.bfloat16, jnp.float32
    return pl.pallas_call(
        functools.partial(attend_kernel, n, math.log2(math.e) / math.sqrt(size)),
        out_shape=jax.ShapeDtypeStruct((heads, rows, size), bf16),
        in_specs=[
            pl.BlockSpec(memory_space=pltpu.VMEM),
            pl.BlockSpec(memory_space=pltpu.VMEM),
            pl.BlockSpec(memory_space=pltpu.VMEM),
        ],
        out_specs=pl.BlockSpec(memory_space=pltpu.VMEM),
        scratch_shapes=[
            pltpu.VMEM((n * rows, size + lanes), bf16),
            pltpu.VMEM((n * rows, size + lanes), bf16),
            pltpu.VMEM((n * rows, 2 * size), bf16),
            pltpu.VMEM((n, 8, lanes), jnp.int32),
            pltpu.VMEM((n, rows, rows), f32),
            pltpu.VMEM((rows, lanes), f32),
            pltpu.VMEM((rows, 2 * size), f32),
            pltpu.VMEM((n, rows, size), bf16),
            pltpu.SemaphoreType.DMA((4, n)),
            pltpu.SemaphoreType.DMA((4, n)),
            pltpu.SemaphoreType.DMA((4,)),
            pltpu.SemaphoreType.DMA((n,)),
            pltpu.SemaphoreType.DMA((n,)),
            pltpu.SemaphoreType.DMA,
        ],
        compiler_params=pltpu.CompilerParams(
            collective_id=0, has_side_effects=True, vmem_limit_bytes=48 * 2**20
        ),
        cost_estimate=pl.CostEstimate(
            flops=5 * n * n * rows * rows * size, bytes_accessed=4 * n * rows * size * 2,
            transcendentals=n * n * rows * rows // 2,
        ),
    )(qkv, clip_rows, bias)


def modulate(activations, mod_table, clip_level, clip_of, clip_count):
    level_count = mod_table.shape[0]
    clip_ids = lax.broadcasted_iota(jnp.int32, (1, clip_count), 1)
    level_ids = lax.broadcasted_iota(jnp.int32, (1, level_count), 1)
    tok_hot = clip_of[:, None] == clip_ids
    level_rows = jnp.sum(jnp.where(tok_hot, clip_level[None, :], 0), axis=1)
    level_hot = (level_rows[:, None] == level_ids).astype(jnp.float32)
    modulation = jnp.dot(level_hot, mod_table, precision=lax.Precision.HIGHEST)
    return (activations.astype(jnp.float32) * (1.0 + modulation)).astype(jnp.bfloat16)


def per_device_heads(
    n, activations, qkv_weight, out_weight, mod_table, clip_level, clip_of, visible
):
    clip_count = visible.shape[0]
    lanes = 128
    moduled = modulate(activations, mod_table, clip_level, clip_of, clip_count)
    qkv = jnp.einsum(
        "td,dchk->chtk", moduled, qkv_weight, preferred_element_type=jnp.float32
    ).astype(jnp.bfloat16)
    clip_rows = clip_of.reshape(-1, lanes)
    clip_rows = jnp.pad(clip_rows, ((0, 8 - clip_rows.shape[0]), (0, 0)))
    bias = jnp.where(visible > 0, 0.0, -(2.0**100)).astype(jnp.bfloat16)
    bias = jnp.pad(bias, ((0, lanes - clip_count), (0, lanes - clip_count)))
    attended = attend_heads(qkv, clip_rows, bias, n)
    return lax.psum_scatter(
        jnp.einsum(
            "htd,hdo->to", attended, out_weight, preferred_element_type=jnp.float32
        ).astype(jnp.bfloat16),
        "head",
        scatter_dimension=0,
        tiled=True,
    )


def solution(mesh):
    placed = (
        P("ctx", None),
        P(None, None, "head", None),
        P("head", None, None),
        P(),
        P(),
        P("ctx"),
        P(),
    )
    n = mesh.shape["ctx"]

    def pick(activations, qkv_weight, out_weight, mod_table, clip_level, clip_of, visible):
        rows, heads, size = clip_of.shape[0], qkv_weight.shape[2], qkv_weight.shape[3]
        fits = heads == n and size == 128 and rows % 128 == 0 and 256 <= rows <= 1024
        fits = fits and visible.shape[0] <= 128
        body = functools.partial(per_device_heads, n) if fits else per_device
        return body(activations, qkv_weight, out_weight, mod_table, clip_level, clip_of, visible)

    return jax.shard_map(
        pick, mesh=mesh, in_specs=placed, out_specs=P(("ctx", "head"), None), check_vma=False
    )
```

```python
import functools
import math

import jax
import jax.numpy as jnp
from jax import lax
from jax.experimental import pallas as pl
from jax.experimental.pallas import tpu as pltpu
from jax.sharding import PartitionSpec as P


def score_block(state_now, kv_block, key_clips, queries, query_vis, score_scale):
    clip_count = query_vis.shape[1]
    clip_ids = lax.broadcasted_iota(jnp.int32, (1, clip_count), 1)
    key_hot = (key_clips[:, None] == clip_ids).astype(jnp.float32)
    allowed = jnp.dot(query_vis, key_hot.T, precision=lax.Precision.HIGHEST) > 0.5
    top_score, totals, summed = state_now
    key_rows = kv_block[:, 0]
    value_rows = kv_block[:, 1]
    scores = (
        jnp.einsum("rhd,khd->hrk", queries, key_rows, preferred_element_type=jnp.float32)
        * score_scale
    )
    masked = jnp.where(allowed[None], scores, -1e30)
    new_top = jnp.maximum(top_score, jnp.max(masked, axis=2))
    weights = jnp.where(allowed[None], jnp.exp(masked - new_top[:, :, None]), 0.0)
    factor = jnp.exp(top_score - new_top)
    totals = totals * factor + jnp.sum(weights, axis=2)
    summed = summed * factor[:, :, None] + jnp.einsum(
        "hrk,khd->hrd", weights.astype(jnp.bfloat16), value_rows, preferred_element_type=jnp.float32
    )
    return (new_top, totals, summed)


def fold_keys(state_now, kv_rows, key_clips, queries, query_vis, score_scale):
    key_count = kv_rows.shape[0]
    block_rows = math.gcd(key_count, 512)

    def one_block(block_index, state_in):
        first_row = block_index * block_rows
        kv_block = lax.dynamic_slice_in_dim(kv_rows, first_row, block_rows, 0)
        clip_block = lax.dynamic_slice_in_dim(key_clips, first_row, block_rows, 0)
        return score_block(state_in, kv_block, clip_block, queries, query_vis, score_scale)

    return lax.fori_loop(0, key_count // block_rows, one_block, state_now)


def per_device(activations, qkv_weight, out_weight, mod_table, clip_level, clip_of, visible):
    heads_here = qkv_weight.shape[2]
    head_size = qkv_weight.shape[3]
    clip_count = visible.shape[0]
    level_count = mod_table.shape[0]
    clip_ids = lax.broadcasted_iota(jnp.int32, (1, clip_count), 1)
    level_ids = lax.broadcasted_iota(jnp.int32, (1, level_count), 1)
    tok_hot = clip_of[:, None] == clip_ids
    level_rows = jnp.sum(jnp.where(tok_hot, clip_level[None, :], 0), axis=1)
    level_hot = (level_rows[:, None] == level_ids).astype(jnp.float32)
    modulation = jnp.dot(level_hot, mod_table, precision=lax.Precision.HIGHEST)
    moduled = (activations.astype(jnp.float32) * (1.0 + modulation)).astype(jnp.bfloat16)
    qkv = jnp.einsum(
        "td,dchk->tchk", moduled, qkv_weight, preferred_element_type=jnp.float32
    ).astype(jnp.bfloat16)
    queries = qkv[:, 0]
    kv_local = qkv[:, 1:3]
    query_count = queries.shape[0]
    query_hot = (clip_of[:, None] == clip_ids).astype(jnp.float32)
    query_vis = jnp.dot(query_hot, visible.astype(jnp.float32), precision=lax.Precision.HIGHEST)
    score_scale = 1.0 / jnp.sqrt(jnp.float32(head_size))
    initial = (
        jnp.full((heads_here, query_count), -1e30, jnp.float32),
        jnp.zeros((heads_here, query_count), jnp.float32),
        jnp.zeros((heads_here, query_count, head_size), jnp.float32),
    )
    kv_all, clips_all = (
        lax.all_gather(kv_local, "ctx", axis=0, tiled=True),
        lax.all_gather(clip_of, "ctx", axis=0, tiled=True),
    )
    final = fold_keys(initial, kv_all, clips_all, queries, query_vis, score_scale)
    attended = (final[2] / final[1][:, :, None]).astype(jnp.bfloat16)
    attended_rows = jnp.transpose(attended, (1, 0, 2))
    return lax.psum_scatter(
        jnp.einsum(
            "rhd,hdo->ro", attended_rows, out_weight, preferred_element_type=jnp.float32
        ).astype(jnp.bfloat16),
        "head",
        scatter_dimension=0,
        tiled=True,
    )


def exchange(sources, targets, sends, recvs, peer):
    return [
        pltpu.make_async_remote_copy(
            src_ref=source,
            dst_ref=target,
            send_sem=send,
            recv_sem=recv,
            device_id={"ctx": peer},
            device_id_type=pl.DeviceIdType.MESH,
        )
        for source, target, send, recv in zip(sources, targets, sends, recvs)
    ]


def attend_kernel(
    n, score_scale, qkv_ref, clip_ref, bias_ref, out_ref,
    query_buf, key_buf, value_buf, clip_buf, score_buf, top_buf, sum_buf, done_buf,
    send_sem, recv_sem, local_sem, back_send, back_recv, back_local,
):
    me = lax.axis_index("ctx")
    rows = qkv_ref.shape[2]
    size = qkv_ref.shape[3]
    lanes = clip_ref.shape[1]

    def span(block):
        return pl.ds(pl.multiple_of(block * rows, rows), rows)

    def landing(owner):
        return [
            query_buf.at[span(owner), pl.ds(0, size)],
            key_buf.at[span(owner), pl.ds(0, size)],
            value_buf.at[span(owner), pl.ds(0, size)],
            clip_buf.at[owner],
        ]

    def leaving(peer):
        return [qkv_ref.at[0, peer], qkv_ref.at[1, peer], qkv_ref.at[2, peer], clip_ref]

    barrier = pltpu.get_barrier_semaphore()
    for step in range(1, n):
        pl.semaphore_signal(
            barrier, inc=1, device_id={"ctx": lax.rem(me + step, n)},
            device_id_type=pl.DeviceIdType.MESH,
        )
    pl.semaphore_wait(barrier, n - 1)

    def outgoing(peer):
        return exchange(
            leaving(peer), landing(me),
            [send_sem.at[item, peer] for item in range(4)],
            [recv_sem.at[item, me] for item in range(4)], peer,
        )

    def incoming(owner):
        return exchange(
            leaving(owner), landing(owner),
            [send_sem.at[item, owner] for item in range(4)],
            [recv_sem.at[item, owner] for item in range(4)], owner,
        )

    def send_step(step, carry):
        for copy in outgoing(lax.rem(me + step, n)):
            copy.start()
        return carry

    lax.fori_loop(1, n, send_step, 0)
    own = [
        pltpu.make_async_copy(source, target, local_sem.at[item])
        for item, (source, target) in enumerate(zip(leaving(me), landing(me)))
    ]
    for copy in own:
        copy.start()
    value_buf[:, size:] = jnp.ones((n * rows, size), value_buf.dtype)
    for copy in own:
        copy.wait()

    def take(owner):
        @pl.when(owner != me)
        def _():
            for copy in incoming(owner):
                copy.wait_recv()

        ids = lax.broadcasted_iota(jnp.int32, (lanes, lanes), 0)
        for part in range(rows // lanes):
            row = clip_buf[owner, pl.ds(part, 1), :]
            hot = jnp.where(ids == row, 1.0, 0.0).T.astype(jnp.bfloat16)
            at = pl.ds(pl.multiple_of(owner * rows + part * lanes, lanes), lanes)
            key_buf[at, size:] = hot
            query_buf[at, size:] = jnp.dot(
                hot, bias_ref[...], preferred_element_type=jnp.float32
            ).astype(jnp.bfloat16)

    def back(block):
        return exchange(
            [done_buf.at[block]], [out_ref.at[me]],
            [back_send.at[block]], [back_recv.at[me]], block,
        )[0]

    def back_in(owner):
        return exchange(
            [done_buf.at[owner]], [out_ref.at[owner]],
            [back_send.at[owner]], [back_recv.at[owner]], owner,
        )[0]

    own_back = pltpu.make_async_copy(done_buf.at[me], out_ref.at[me], back_local)
    take(0)

    def one_block(block, carry):
        @pl.when(block < n - 1)
        def _():
            take(block + 1)

        count = jnp.minimum(block + 2, n)
        top_buf[...] = jnp.full(top_buf.shape, -jnp.inf, jnp.float32)

        def score(at, inner):
            found = lax.dot_general(
                query_buf[span(block), :], key_buf[span(at), :],
                (((1,), (1,)), ((), ())), preferred_element_type=jnp.float32,
            )
            score_buf[at] = found
            top = top_buf[...]
            for part in range(rows // lanes):
                top = jnp.maximum(top, found[:, part * lanes : (part + 1) * lanes])
            top_buf[...] = top
            return inner

        lax.fori_loop(0, count, score, 0)
        highest = jnp.max(top_buf[...], axis=1, keepdims=True) * score_scale
        top_buf[...] = jnp.broadcast_to(highest, top_buf.shape)
        sum_buf[...] = jnp.zeros(sum_buf.shape, jnp.float32)

        def weigh(at, inner):
            top = top_buf[...]
            weights = jnp.concatenate(
                [
                    jnp.exp2(
                        score_buf[at, :, part * lanes : (part + 1) * lanes] * score_scale - top
                    ).astype(jnp.bfloat16)
                    for part in range(rows // lanes)
                ],
                axis=1,
            )
            sum_buf[...] += jnp.dot(
                weights, value_buf[span(at), :], preferred_element_type=jnp.float32
            )
            return inner

        lax.fori_loop(0, count, weigh, 0)
        done_buf[block] = (sum_buf[:, :size] / sum_buf[:, size:]).astype(jnp.bfloat16)

        @pl.when(block != me)
        def _():
            back(block).start()

        @pl.when(block == me)
        def _():
            own_back.start()

        return carry

    lax.fori_loop(0, n, one_block, 0)

    def finish(step, carry):
        peer = lax.rem(me + step, n)
        for copy in outgoing(peer):
            copy.wait_send()
        back(peer).wait_send()
        back_in(peer).wait_recv()
        return carry

    lax.fori_loop(1, n, finish, 0)
    own_back.wait()


def attend_heads(qkv, clip_rows, bias, n):
    _, heads, rows, size = qkv.shape
    lanes = clip_rows.shape[1]
    bf16, f32 = jnp.bfloat16, jnp.float32
    return pl.pallas_call(
        functools.partial(attend_kernel, n, math.log2(math.e) / math.sqrt(size)),
        out_shape=jax.ShapeDtypeStruct((heads, rows, size), bf16),
        in_specs=[
            pl.BlockSpec(memory_space=pltpu.VMEM),
            pl.BlockSpec(memory_space=pltpu.VMEM),
            pl.BlockSpec(memory_space=pltpu.VMEM),
        ],
        out_specs=pl.BlockSpec(memory_space=pltpu.VMEM),
        scratch_shapes=[
            pltpu.VMEM((n * rows, size + lanes), bf16),
            pltpu.VMEM((n * rows, size + lanes), bf16),
            pltpu.VMEM((n * rows, 2 * size), bf16),
            pltpu.VMEM((n, 8, lanes), jnp.int32),
            pltpu.VMEM((n, rows, rows), f32),
            pltpu.VMEM((rows, lanes), f32),
            pltpu.VMEM((rows, 2 * size), f32),
            pltpu.VMEM((n, rows, size), bf16),
            pltpu.SemaphoreType.DMA((4, n)),
            pltpu.SemaphoreType.DMA((4, n)),
            pltpu.SemaphoreType.DMA((4,)),
            pltpu.SemaphoreType.DMA((n,)),
            pltpu.SemaphoreType.DMA((n,)),
            pltpu.SemaphoreType.DMA,
        ],
        compiler_params=pltpu.CompilerParams(
            collective_id=0, has_side_effects=True, vmem_limit_bytes=48 * 2**20
        ),
        cost_estimate=pl.CostEstimate(
            flops=5 * n * n * rows * rows * size, bytes_accessed=4 * n * rows * size * 2,
            transcendentals=n * n * rows * rows // 2,
        ),
    )(qkv, clip_rows, bias)


def project_kernel(
    pieces, attended_ref, weight_ref, out_ref,
    part_buf, send_buf, up_buf, down_buf, send_sem, up_sem, down_sem,
):
    plane = lax.axis_index("head")
    last = part_buf.shape[0] - 1
    rows = part_buf.shape[1]
    width = part_buf.shape[2] // pieces
    heads, size, _ = weight_ref.shape
    middle = (plane > 0) & (plane < last)

    def columns(piece):
        return pl.ds(pl.multiple_of(piece * width, width), width)

    barrier = pltpu.get_barrier_semaphore()

    @pl.when(plane > 0)
    def _():
        pl.semaphore_signal(
            barrier, inc=1, device_id={"head": plane - 1}, device_id_type=pl.DeviceIdType.MESH
        )

    @pl.when(plane < last)
    def _():
        pl.semaphore_signal(
            barrier, inc=1, device_id={"head": plane + 1}, device_id_type=pl.DeviceIdType.MESH
        )

    @pl.when(middle)
    def _():
        pl.semaphore_wait(barrier, 2)

    @pl.when(jnp.logical_not(middle))
    def _():
        pl.semaphore_wait(barrier, 1)

    def upward(share, piece, peer):
        return pltpu.make_async_remote_copy(
            src_ref=send_buf.at[share, :, columns(piece)],
            dst_ref=up_buf.at[share, :, columns(piece)],
            send_sem=send_sem.at[share, piece],
            recv_sem=up_sem.at[share, piece],
            device_id={"head": peer},
            device_id_type=pl.DeviceIdType.MESH,
        )

    def downward(share, piece, peer):
        return pltpu.make_async_remote_copy(
            src_ref=send_buf.at[share, :, columns(piece)],
            dst_ref=down_buf.at[share, :, columns(piece)],
            send_sem=send_sem.at[share, piece],
            recv_sem=down_sem.at[share, piece],
            device_id={"head": peer},
            device_id_type=pl.DeviceIdType.MESH,
        )

    near = jnp.where(plane == 0, 1, plane - 1)
    low = jnp.minimum(plane, last - plane)

    def compute(step, carry):
        order, piece = step // pieces, lax.rem(step, pieces)
        ahead = last - low
        mirrored = jnp.where(order < ahead, last - order, order - ahead)
        share = jnp.where(plane + plane < last, mirrored, last - mirrored)
        at = pl.ds(pl.multiple_of(share * rows, rows), rows)
        left = jnp.concatenate([attended_ref[head, at, :] for head in range(heads)], axis=1)
        right = weight_ref[:, :, columns(piece)].reshape(heads * size, width)
        part = jnp.dot(left, right, preferred_element_type=jnp.float32)
        part_buf[share, :, columns(piece)] = part

        @pl.when((plane == 0) & (share > 0))
        def _():
            send_buf[share, :, columns(piece)] = part.astype(jnp.bfloat16)
            upward(share, piece, plane + 1).start()

        @pl.when((plane == last) & (share < last))
        def _():
            send_buf[share, :, columns(piece)] = part.astype(jnp.bfloat16)
            downward(share, piece, plane - 1).start()

        return carry

    lax.fori_loop(0, (last + 1) * pieces, compute, 0)

    def relay_up(share, piece):
        upward(share, piece, near).wait_recv()
        total = part_buf[share, :, columns(piece)] + up_buf[share, :, columns(piece)].astype(
            jnp.float32
        )
        send_buf[share, :, columns(piece)] = total.astype(jnp.bfloat16)
        upward(share, piece, plane + 1).start()

    def relay_down(share, piece):
        downward(share, piece, near).wait_recv()
        total = part_buf[share, :, columns(piece)] + down_buf[share, :, columns(piece)].astype(
            jnp.float32
        )
        send_buf[share, :, columns(piece)] = total.astype(jnp.bfloat16)
        downward(share, piece, plane - 1).start()

    @pl.when(middle)
    def _():
        def relay(step, carry):
            order, piece = step // pieces, lax.rem(step, pieces)

            @pl.when(order < last - plane)
            def _():
                relay_up(last - order, piece)

            @pl.when(order < plane)
            def _():
                relay_down(order, piece)

            return carry

        lax.fori_loop(0, (last - 1) * pieces, relay, 0)

    def settle(piece, carry):
        part_now = part_buf[plane, :, columns(piece)]

        @pl.when(plane == 0)
        def _():
            downward(plane, piece, near).wait_recv()
            total = part_now + down_buf[plane, :, columns(piece)].astype(jnp.float32)
            out_ref[:, columns(piece)] = total.astype(jnp.bfloat16)

        @pl.when(plane == last)
        def _():
            upward(plane, piece, near).wait_recv()
            total = part_now + up_buf[plane, :, columns(piece)].astype(jnp.float32)
            out_ref[:, columns(piece)] = total.astype(jnp.bfloat16)

        @pl.when(middle)
        def _():
            upward(plane, piece, near).wait_recv()
            downward(plane, piece, near).wait_recv()
            total = (
                part_now
                + up_buf[plane, :, columns(piece)].astype(jnp.float32)
                + down_buf[plane, :, columns(piece)].astype(jnp.float32)
            )
            out_ref[:, columns(piece)] = total.astype(jnp.bfloat16)

        return carry

    lax.fori_loop(0, pieces, settle, 0)

    def finish(step, carry):
        share, piece = step // pieces, lax.rem(step, pieces)

        @pl.when(share != plane)
        def _():
            upward(share, piece, near).wait_send()

        return carry

    lax.fori_loop(0, (last + 1) * pieces, finish, 0)


def project_heads(attended, out_weight, planes):
    heads, rows, size = attended.shape
    model = out_weight.shape[2]
    share = rows // planes
    pieces = 8
    bf16 = jnp.bfloat16
    return pl.pallas_call(
        functools.partial(project_kernel, pieces),
        out_shape=jax.ShapeDtypeStruct((share, model), bf16),
        in_specs=[pl.BlockSpec(memory_space=pltpu.VMEM)] * 2,
        out_specs=pl.BlockSpec(memory_space=pltpu.VMEM),
        scratch_shapes=[
            pltpu.VMEM((planes, share, model), jnp.float32),
            pltpu.VMEM((planes, share, model), bf16),
            pltpu.VMEM((planes, share, model), bf16),
            pltpu.VMEM((planes, share, model), bf16),
            pltpu.SemaphoreType.DMA((planes, pieces)),
            pltpu.SemaphoreType.DMA((planes, pieces)),
            pltpu.SemaphoreType.DMA((planes, pieces)),
        ],
        compiler_params=pltpu.CompilerParams(
            collective_id=1, has_side_effects=True, vmem_limit_bytes=48 * 2**20
        ),
        cost_estimate=pl.CostEstimate(
            flops=2 * rows * heads * size * model,
            bytes_accessed=2 * heads * size * (model + rows),
            transcendentals=0,
        ),
    )(attended, out_weight)


def modulate(activations, mod_table, clip_level, clip_of, clip_count):
    level_count = mod_table.shape[0]
    clip_ids = lax.broadcasted_iota(jnp.int32, (1, clip_count), 1)
    level_ids = lax.broadcasted_iota(jnp.int32, (1, level_count), 1)
    tok_hot = clip_of[:, None] == clip_ids
    level_rows = jnp.sum(jnp.where(tok_hot, clip_level[None, :], 0), axis=1)
    level_hot = (level_rows[:, None] == level_ids).astype(jnp.float32)
    modulation = jnp.dot(level_hot, mod_table, precision=lax.Precision.HIGHEST)
    return (activations.astype(jnp.float32) * (1.0 + modulation)).astype(jnp.bfloat16)


def per_device_heads(
    n, planes, activations, qkv_weight, out_weight, mod_table, clip_level, clip_of, visible
):
    clip_count = visible.shape[0]
    lanes = 128
    moduled = modulate(activations, mod_table, clip_level, clip_of, clip_count)
    qkv = jnp.einsum(
        "td,dchk->chtk", moduled, qkv_weight, preferred_element_type=jnp.float32
    ).astype(jnp.bfloat16)
    clip_rows = clip_of.reshape(-1, lanes)
    clip_rows = jnp.pad(clip_rows, ((0, 8 - clip_rows.shape[0]), (0, 0)))
    bias = jnp.where(visible > 0, 0.0, -(2.0**100)).astype(jnp.bfloat16)
    bias = jnp.pad(bias, ((0, lanes - clip_count), (0, lanes - clip_count)))
    attended = attend_heads(qkv, clip_rows, bias, n)
    return project_heads(attended, out_weight, planes)


def solution(mesh):
    placed = (
        P("ctx", None),
        P(None, None, "head", None),
        P("head", None, None),
        P(),
        P(),
        P("ctx"),
        P(),
    )
    n, planes = mesh.shape["ctx"], mesh.shape["head"]

    def pick(activations, qkv_weight, out_weight, mod_table, clip_level, clip_of, visible):
        rows, heads, size = clip_of.shape[0], qkv_weight.shape[2], qkv_weight.shape[3]
        fits = heads == n and size == 128 and rows % 128 == 0 and 256 <= rows <= 1024
        fits = fits and visible.shape[0] <= 128 and planes == 4
        fits = fits and out_weight.shape[2] % 1024 == 0
        body = functools.partial(per_device_heads, n, planes) if fits else per_device
        return body(activations, qkv_weight, out_weight, mod_table, clip_level, clip_of, visible)

    return jax.shard_map(
        pick, mesh=mesh, in_specs=placed, out_specs=P(("ctx", "head"), None), check_vma=False
    )
```

```python
import functools
import math

import jax
import jax.numpy as jnp
from jax import lax
from jax.experimental import pallas as pl
from jax.experimental.pallas import tpu as pltpu
from jax.sharding import PartitionSpec as P


def score_block(state_now, kv_block, key_clips, queries, query_vis, score_scale):
    clip_count = query_vis.shape[1]
    clip_ids = lax.broadcasted_iota(jnp.int32, (1, clip_count), 1)
    key_hot = (key_clips[:, None] == clip_ids).astype(jnp.float32)
    allowed = jnp.dot(query_vis, key_hot.T, precision=lax.Precision.HIGHEST) > 0.5
    top_score, totals, summed = state_now
    key_rows = kv_block[:, 0]
    value_rows = kv_block[:, 1]
    scores = (
        jnp.einsum("rhd,khd->hrk", queries, key_rows, preferred_element_type=jnp.float32)
        * score_scale
    )
    masked = jnp.where(allowed[None], scores, -1e30)
    new_top = jnp.maximum(top_score, jnp.max(masked, axis=2))
    weights = jnp.where(allowed[None], jnp.exp(masked - new_top[:, :, None]), 0.0)
    factor = jnp.exp(top_score - new_top)
    totals = totals * factor + jnp.sum(weights, axis=2)
    summed = summed * factor[:, :, None] + jnp.einsum(
        "hrk,khd->hrd", weights.astype(jnp.bfloat16), value_rows, preferred_element_type=jnp.float32
    )
    return (new_top, totals, summed)


def fold_keys(state_now, kv_rows, key_clips, queries, query_vis, score_scale):
    key_count = kv_rows.shape[0]
    block_rows = math.gcd(key_count, 512)

    def one_block(block_index, state_in):
        first_row = block_index * block_rows
        kv_block = lax.dynamic_slice_in_dim(kv_rows, first_row, block_rows, 0)
        clip_block = lax.dynamic_slice_in_dim(key_clips, first_row, block_rows, 0)
        return score_block(state_in, kv_block, clip_block, queries, query_vis, score_scale)

    return lax.fori_loop(0, key_count // block_rows, one_block, state_now)


def per_device(activations, qkv_weight, out_weight, mod_table, clip_level, clip_of, visible):
    heads_here = qkv_weight.shape[2]
    head_size = qkv_weight.shape[3]
    clip_count = visible.shape[0]
    level_count = mod_table.shape[0]
    clip_ids = lax.broadcasted_iota(jnp.int32, (1, clip_count), 1)
    level_ids = lax.broadcasted_iota(jnp.int32, (1, level_count), 1)
    tok_hot = clip_of[:, None] == clip_ids
    level_rows = jnp.sum(jnp.where(tok_hot, clip_level[None, :], 0), axis=1)
    level_hot = (level_rows[:, None] == level_ids).astype(jnp.float32)
    modulation = jnp.dot(level_hot, mod_table, precision=lax.Precision.HIGHEST)
    moduled = (activations.astype(jnp.float32) * (1.0 + modulation)).astype(jnp.bfloat16)
    qkv = jnp.einsum(
        "td,dchk->tchk", moduled, qkv_weight, preferred_element_type=jnp.float32
    ).astype(jnp.bfloat16)
    queries = qkv[:, 0]
    kv_local = qkv[:, 1:3]
    query_count = queries.shape[0]
    query_hot = (clip_of[:, None] == clip_ids).astype(jnp.float32)
    query_vis = jnp.dot(query_hot, visible.astype(jnp.float32), precision=lax.Precision.HIGHEST)
    score_scale = 1.0 / jnp.sqrt(jnp.float32(head_size))
    initial = (
        jnp.full((heads_here, query_count), -1e30, jnp.float32),
        jnp.zeros((heads_here, query_count), jnp.float32),
        jnp.zeros((heads_here, query_count, head_size), jnp.float32),
    )
    kv_all, clips_all = (
        lax.all_gather(kv_local, "ctx", axis=0, tiled=True),
        lax.all_gather(clip_of, "ctx", axis=0, tiled=True),
    )
    final = fold_keys(initial, kv_all, clips_all, queries, query_vis, score_scale)
    attended = (final[2] / final[1][:, :, None]).astype(jnp.bfloat16)
    attended_rows = jnp.transpose(attended, (1, 0, 2))
    return lax.psum_scatter(
        jnp.einsum(
            "rhd,hdo->ro", attended_rows, out_weight, preferred_element_type=jnp.float32
        ).astype(jnp.bfloat16),
        "head",
        scatter_dimension=0,
        tiled=True,
    )


def exchange(sources, targets, sends, recvs, peer):
    return [
        pltpu.make_async_remote_copy(
            src_ref=source,
            dst_ref=target,
            send_sem=send,
            recv_sem=recv,
            device_id={"ctx": peer},
            device_id_type=pl.DeviceIdType.MESH,
        )
        for source, target, send, recv in zip(sources, targets, sends, recvs)
    ]


def attend_kernel(
    n, score_scale, planes, half, *refs
):
    if half == 0:
        qkv_ref, clip_ref, bias_ref, out_ref, query_buf, key_buf, value_buf, *scratch = refs
        clip_buf, send_sem, recv_sem, local_sem, *scratch = scratch
    else:
        query_buf, key_buf, value_buf, out_ref, *scratch = refs
    score_buf, top_buf, sum_buf, done_buf, back_send, back_recv, back_local = scratch
    me = lax.axis_index("ctx")
    rows = query_buf.shape[0] // n
    size = value_buf.shape[1] // 2
    lanes = top_buf.shape[1]
    group = rows // planes

    def span(block):
        return pl.ds(pl.multiple_of(block * rows, rows), rows)

    def landing(owner):
        return [
            query_buf.at[span(owner), pl.ds(0, size)],
            key_buf.at[span(owner), pl.ds(0, size)],
            value_buf.at[span(owner), pl.ds(0, size)],
            clip_buf.at[owner],
        ]

    def leaving(peer):
        return [qkv_ref.at[0, peer], qkv_ref.at[1, peer], qkv_ref.at[2, peer], clip_ref]

    barrier = pltpu.get_barrier_semaphore()
    for step in range(1, n):
        pl.semaphore_signal(
            barrier, inc=1, device_id={"ctx": lax.rem(me + step, n)},
            device_id_type=pl.DeviceIdType.MESH,
        )
    pl.semaphore_wait(barrier, n - 1)

    def outgoing(peer):
        return exchange(
            leaving(peer), landing(me),
            [send_sem.at[item, peer] for item in range(4)],
            [recv_sem.at[item, me] for item in range(4)], peer,
        )

    def incoming(owner):
        return exchange(
            leaving(owner), landing(owner),
            [send_sem.at[item, owner] for item in range(4)],
            [recv_sem.at[item, owner] for item in range(4)], owner,
        )

    def send_step(step, carry):
        for copy in outgoing(lax.rem(me + step, n)):
            copy.start()
        return carry

    if half == 0:
        lax.fori_loop(1, n, send_step, 0)
        own = [
            pltpu.make_async_copy(source, target, local_sem.at[item])
            for item, (source, target) in enumerate(zip(leaving(me), landing(me)))
        ]
        for copy in own:
            copy.start()
        value_buf[:, size:] = jnp.ones((n * rows, size), value_buf.dtype)
        for copy in own:
            copy.wait()

    def take(owner):
        @pl.when(owner != me)
        def _():
            for copy in incoming(owner):
                copy.wait_recv()

        ids = lax.broadcasted_iota(jnp.int32, (lanes, lanes), 0)
        for part in range(rows // lanes):
            row = clip_buf[owner, pl.ds(part, 1), :]
            hot = jnp.where(ids == row, 1.0, 0.0).T.astype(jnp.bfloat16)
            at = pl.ds(pl.multiple_of(owner * rows + part * lanes, lanes), lanes)
            key_buf[at, size:] = hot
            query_buf[at, size:] = jnp.dot(
                hot, bias_ref[...], preferred_element_type=jnp.float32
            ).astype(jnp.bfloat16)

    def back(block):
        return exchange(
            [done_buf.at[block]], [out_ref.at[me]],
            [back_send.at[block]], [back_recv.at[me]], block,
        )[0]

    def back_in(owner):
        return exchange(
            [done_buf.at[owner]], [out_ref.at[owner]],
            [back_send.at[owner]], [back_recv.at[owner]], owner,
        )[0]

    own_back = pltpu.make_async_copy(done_buf.at[me], out_ref.at[me], back_local)
    if half == 0:
        take(0)

    def one_block(block, carry):
        if half == 0:
            @pl.when(block < n - 1)
            def _():
                take(block + 1)

        starts = [
            pl.multiple_of(block * rows + plane * group + half * (group // 2), group // 2)
            for plane in range(planes)
        ]
        mine = jnp.concatenate(
            [query_buf[pl.ds(start, group // 2), :] for start in starts], axis=0
        )

        count = jnp.minimum(block + 2, n)
        top_buf[...] = jnp.full(top_buf.shape, -jnp.inf, jnp.float32)

        def score(at, inner):
            found = lax.dot_general(
                mine, key_buf[span(at), :],
                (((1,), (1,)), ((), ())), preferred_element_type=jnp.float32,
            )
            score_buf[at] = found
            top = top_buf[...]
            for part in range(rows // lanes):
                top = jnp.maximum(top, found[:, part * lanes : (part + 1) * lanes])
            top_buf[...] = top
            return inner

        lax.fori_loop(0, count, score, 0)
        highest = jnp.max(top_buf[...], axis=1, keepdims=True) * score_scale
        top_buf[...] = jnp.broadcast_to(highest, top_buf.shape)
        sum_buf[...] = jnp.zeros(sum_buf.shape, jnp.float32)

        def weigh(at, inner):
            top = top_buf[...]
            weights = jnp.concatenate(
                [
                    jnp.exp2(
                        score_buf[at, :, part * lanes : (part + 1) * lanes] * score_scale - top
                    ).astype(jnp.bfloat16)
                    for part in range(rows // lanes)
                ],
                axis=1,
            )
            sum_buf[...] += jnp.dot(
                weights, value_buf[span(at), :], preferred_element_type=jnp.float32
            )
            return inner

        lax.fori_loop(0, count, weigh, 0)
        done_buf[block] = (sum_buf[:, :size] / sum_buf[:, size:]).astype(jnp.bfloat16)

        @pl.when(block != me)
        def _():
            back(block).start()

        @pl.when(block == me)
        def _():
            own_back.start()

        return carry

    lax.fori_loop(0, n, one_block, 0)

    def finish(step, carry):
        peer = lax.rem(me + step, n)
        if half == 0:
            for copy in outgoing(peer):
                copy.wait_send()
        back(peer).wait_send()
        back_in(peer).wait_recv()
        return carry

    lax.fori_loop(1, n, finish, 0)
    own_back.wait()


def attend_half(operands, n, planes, half, rows, size):
    lanes, few = 128, rows // 2
    bf16, f32 = jnp.bfloat16, jnp.float32
    held = [jax.ShapeDtypeStruct((n * rows, 2 * size), bf16)] * 3
    outs = [jax.ShapeDtypeStruct((n, few, size), bf16)] + (held if half == 0 else [])
    exchanged = [
        pltpu.VMEM((n, 8, lanes), jnp.int32),
        pltpu.SemaphoreType.DMA((4, n)),
        pltpu.SemaphoreType.DMA((4, n)),
        pltpu.SemaphoreType.DMA((4,)),
    ]
    scale = math.log2(math.e) / math.sqrt(size)
    return pl.pallas_call(
        functools.partial(attend_kernel, n, scale, planes, half),
        out_shape=outs,
        in_specs=[pl.BlockSpec(memory_space=pltpu.VMEM)] * len(operands),
        out_specs=[pl.BlockSpec(memory_space=pltpu.VMEM)] * len(outs),
        scratch_shapes=(exchanged if half == 0 else [])
        + [
            pltpu.VMEM((n, few, rows), f32),
            pltpu.VMEM((few, lanes), f32),
            pltpu.VMEM((few, 2 * size), f32),
            pltpu.VMEM((n, few, size), bf16),
            pltpu.SemaphoreType.DMA((n,)),
            pltpu.SemaphoreType.DMA((n,)),
            pltpu.SemaphoreType.DMA,
        ],
        compiler_params=pltpu.CompilerParams(
            collective_id=half, has_side_effects=True, vmem_limit_bytes=40 * 2**20
        ),
        cost_estimate=pl.CostEstimate(
            flops=3 * n * n * rows * rows * size, bytes_accessed=4 * n * rows * size * 2,
            transcendentals=n * n * rows * rows // 4,
        ),
    )(*operands)


def modulate(activations, mod_table, clip_level, clip_of, clip_count):
    level_count = mod_table.shape[0]
    clip_ids = lax.broadcasted_iota(jnp.int32, (1, clip_count), 1)
    level_ids = lax.broadcasted_iota(jnp.int32, (1, level_count), 1)
    tok_hot = clip_of[:, None] == clip_ids
    level_rows = jnp.sum(jnp.where(tok_hot, clip_level[None, :], 0), axis=1)
    level_hot = (level_rows[:, None] == level_ids).astype(jnp.float32)
    modulation = jnp.dot(level_hot, mod_table, precision=lax.Precision.HIGHEST)
    return (activations.astype(jnp.float32) * (1.0 + modulation)).astype(jnp.bfloat16)


def per_device_heads(
    n, planes, activations, qkv_weight, out_weight, mod_table, clip_level, clip_of, visible
):
    clip_count = visible.shape[0]
    lanes = 128
    moduled = modulate(activations, mod_table, clip_level, clip_of, clip_count)
    qkv = jnp.einsum(
        "td,dchk->chtk", moduled, qkv_weight, preferred_element_type=jnp.float32
    ).astype(jnp.bfloat16)
    clip_rows = clip_of.reshape(-1, lanes)
    clip_rows = jnp.pad(clip_rows, ((0, 8 - clip_rows.shape[0]), (0, 0)))
    bias = jnp.where(visible > 0, 0.0, -(2.0**100)).astype(jnp.bfloat16)
    bias = jnp.pad(bias, ((0, lanes - clip_count), (0, lanes - clip_count)))
    rows, size = qkv.shape[2:]

    def project(attended):
        return jnp.einsum(
            "htd,hdo->to", attended, out_weight, preferred_element_type=jnp.float32
        ).astype(jnp.bfloat16)

    attended, *held = attend_half([qkv, clip_rows, bias], n, planes, 0, rows, size)
    held, first = lax.optimization_barrier((held, project(attended)))
    first = lax.psum_scatter(first, "head", scatter_dimension=0, tiled=True)
    (attended,) = attend_half(held, n, planes, 1, rows, size)
    second = lax.psum_scatter(project(attended), "head", scatter_dimension=0, tiled=True)
    return jnp.concatenate([first, second], axis=0)


def solution(mesh):
    placed = (
        P("ctx", None),
        P(None, None, "head", None),
        P("head", None, None),
        P(),
        P(),
        P("ctx"),
        P(),
    )
    n, planes = mesh.shape["ctx"], mesh.shape["head"]

    def pick(activations, qkv_weight, out_weight, mod_table, clip_level, clip_of, visible):
        rows, heads, size = clip_of.shape[0], qkv_weight.shape[2], qkv_weight.shape[3]
        fits = heads == n and size == 128 and rows % 128 == 0 and 256 <= rows <= 1024
        fits = fits and visible.shape[0] <= 128 and rows % (32 * planes) == 0
        body = functools.partial(per_device_heads, n, planes) if fits else per_device
        return body(activations, qkv_weight, out_weight, mod_table, clip_level, clip_of, visible)

    return jax.shard_map(
        pick, mesh=mesh, in_specs=placed, out_specs=P(("ctx", "head"), None), check_vma=False
    )
```

```python
import functools
import math

import jax
import jax.numpy as jnp
from jax import lax
from jax.experimental import pallas as pl
from jax.experimental.pallas import tpu as pltpu
from jax.sharding import PartitionSpec as P


def score_block(state_now, kv_block, key_clips, queries, query_vis, score_scale):
    clip_count = query_vis.shape[1]
    clip_ids = lax.broadcasted_iota(jnp.int32, (1, clip_count), 1)
    key_hot = (key_clips[:, None] == clip_ids).astype(jnp.float32)
    allowed = jnp.dot(query_vis, key_hot.T, precision=lax.Precision.HIGHEST) > 0.5
    top_score, totals, summed = state_now
    key_rows = kv_block[:, 0]
    value_rows = kv_block[:, 1]
    scores = (
        jnp.einsum("rhd,khd->hrk", queries, key_rows, preferred_element_type=jnp.float32)
        * score_scale
    )
    masked = jnp.where(allowed[None], scores, -1e30)
    new_top = jnp.maximum(top_score, jnp.max(masked, axis=2))
    weights = jnp.where(allowed[None], jnp.exp(masked - new_top[:, :, None]), 0.0)
    factor = jnp.exp(top_score - new_top)
    totals = totals * factor + jnp.sum(weights, axis=2)
    summed = summed * factor[:, :, None] + jnp.einsum(
        "hrk,khd->hrd", weights.astype(jnp.bfloat16), value_rows, preferred_element_type=jnp.float32
    )
    return (new_top, totals, summed)


def fold_keys(state_now, kv_rows, key_clips, queries, query_vis, score_scale):
    key_count = kv_rows.shape[0]
    block_rows = math.gcd(key_count, 512)

    def one_block(block_index, state_in):
        first_row = block_index * block_rows
        kv_block = lax.dynamic_slice_in_dim(kv_rows, first_row, block_rows, 0)
        clip_block = lax.dynamic_slice_in_dim(key_clips, first_row, block_rows, 0)
        return score_block(state_in, kv_block, clip_block, queries, query_vis, score_scale)

    return lax.fori_loop(0, key_count // block_rows, one_block, state_now)


def per_device(activations, qkv_weight, out_weight, mod_table, clip_level, clip_of, visible):
    heads_here = qkv_weight.shape[2]
    head_size = qkv_weight.shape[3]
    clip_count = visible.shape[0]
    level_count = mod_table.shape[0]
    clip_ids = lax.broadcasted_iota(jnp.int32, (1, clip_count), 1)
    level_ids = lax.broadcasted_iota(jnp.int32, (1, level_count), 1)
    tok_hot = clip_of[:, None] == clip_ids
    level_rows = jnp.sum(jnp.where(tok_hot, clip_level[None, :], 0), axis=1)
    level_hot = (level_rows[:, None] == level_ids).astype(jnp.float32)
    modulation = jnp.dot(level_hot, mod_table, precision=lax.Precision.HIGHEST)
    moduled = (activations.astype(jnp.float32) * (1.0 + modulation)).astype(jnp.bfloat16)
    qkv = jnp.einsum(
        "td,dchk->tchk", moduled, qkv_weight, preferred_element_type=jnp.float32
    ).astype(jnp.bfloat16)
    queries = qkv[:, 0]
    kv_local = qkv[:, 1:3]
    query_count = queries.shape[0]
    query_hot = (clip_of[:, None] == clip_ids).astype(jnp.float32)
    query_vis = jnp.dot(query_hot, visible.astype(jnp.float32), precision=lax.Precision.HIGHEST)
    score_scale = 1.0 / jnp.sqrt(jnp.float32(head_size))
    initial = (
        jnp.full((heads_here, query_count), -1e30, jnp.float32),
        jnp.zeros((heads_here, query_count), jnp.float32),
        jnp.zeros((heads_here, query_count, head_size), jnp.float32),
    )
    kv_all, clips_all = (
        lax.all_gather(kv_local, "ctx", axis=0, tiled=True),
        lax.all_gather(clip_of, "ctx", axis=0, tiled=True),
    )
    final = fold_keys(initial, kv_all, clips_all, queries, query_vis, score_scale)
    attended = (final[2] / final[1][:, :, None]).astype(jnp.bfloat16)
    attended_rows = jnp.transpose(attended, (1, 0, 2))
    return lax.psum_scatter(
        jnp.einsum(
            "rhd,hdo->ro", attended_rows, out_weight, preferred_element_type=jnp.float32
        ).astype(jnp.bfloat16),
        "head",
        scatter_dimension=0,
        tiled=True,
    )


def exchange(sources, targets, sends, recvs, peer):
    return [
        pltpu.make_async_remote_copy(
            src_ref=source,
            dst_ref=target,
            send_sem=send,
            recv_sem=recv,
            device_id={"ctx": peer},
            device_id_type=pl.DeviceIdType.MESH,
        )
        for source, target, send, recv in zip(sources, targets, sends, recvs)
    ]


def attend_kernel(
    n, score_scale, qkv_ref, clip_ref, bias_ref, out_ref,
    query_buf, key_buf, value_buf, clip_buf, score_buf, top_buf, sum_buf, done_buf,
    send_sem, recv_sem, local_sem, back_send, back_recv, back_local,
):
    me = lax.axis_index("ctx")
    rows = qkv_ref.shape[2]
    size = qkv_ref.shape[3]
    lanes = clip_ref.shape[1]

    def span(block):
        return pl.ds(pl.multiple_of(block * rows, rows), rows)

    def landing(owner):
        return [
            query_buf.at[span(owner), pl.ds(0, size)],
            key_buf.at[span(owner), pl.ds(0, size)],
            value_buf.at[span(owner), pl.ds(0, size)],
            clip_buf.at[owner],
        ]

    def leaving(peer):
        return [qkv_ref.at[0, peer], qkv_ref.at[1, peer], qkv_ref.at[2, peer], clip_ref]

    barrier = pltpu.get_barrier_semaphore()
    for step in range(1, n):
        pl.semaphore_signal(
            barrier, inc=1, device_id={"ctx": lax.rem(me + step, n)},
            device_id_type=pl.DeviceIdType.MESH,
        )
    pl.semaphore_wait(barrier, n - 1)

    def outgoing(peer):
        return exchange(
            leaving(peer), landing(me),
            [send_sem.at[item, peer] for item in range(4)],
            [recv_sem.at[item, me] for item in range(4)], peer,
        )

    def incoming(owner):
        return exchange(
            leaving(owner), landing(owner),
            [send_sem.at[item, owner] for item in range(4)],
            [recv_sem.at[item, owner] for item in range(4)], owner,
        )

    def send_step(step, carry):
        for copy in outgoing(lax.rem(me + step, n)):
            copy.start()
        return carry

    lax.fori_loop(1, n, send_step, 0)
    own = [
        pltpu.make_async_copy(source, target, local_sem.at[item])
        for item, (source, target) in enumerate(zip(leaving(me), landing(me)))
    ]
    for copy in own:
        copy.start()
    value_buf[:, size:] = jnp.ones((n * rows, size), value_buf.dtype)
    for copy in own:
        copy.wait()

    def take(owner):
        @pl.when(owner != me)
        def _():
            for copy in incoming(owner):
                copy.wait_recv()

        ids = lax.broadcasted_iota(jnp.int32, (lanes, lanes), 0)
        for part in range(rows // lanes):
            row = clip_buf[owner, pl.ds(part, 1), :]
            hot = jnp.where(ids == row, 1.0, 0.0).T.astype(jnp.bfloat16)
            at = pl.ds(pl.multiple_of(owner * rows + part * lanes, lanes), lanes)
            key_buf[at, size:] = hot
            query_buf[at, size:] = jnp.dot(
                hot, bias_ref[...], preferred_element_type=jnp.float32
            ).astype(jnp.bfloat16)

    def back(block):
        return exchange(
            [done_buf.at[block]], [out_ref.at[me]],
            [back_send.at[block]], [back_recv.at[me]], block,
        )[0]

    def back_in(owner):
        return exchange(
            [done_buf.at[owner]], [out_ref.at[owner]],
            [back_send.at[owner]], [back_recv.at[owner]], owner,
        )[0]

    own_back = pltpu.make_async_copy(done_buf.at[me], out_ref.at[me], back_local)
    take(0)

    def one_block(block, carry):
        @pl.when(block < n - 1)
        def _():
            take(block + 1)

        count = jnp.minimum(block + 2, n)
        top_buf[...] = jnp.full(top_buf.shape, -jnp.inf, jnp.float32)

        def score(at, inner):
            found = lax.dot_general(
                query_buf[span(block), :], key_buf[span(at), :],
                (((1,), (1,)), ((), ())), preferred_element_type=jnp.float32,
            )
            score_buf[at] = found
            top = top_buf[...]
            for part in range(rows // lanes):
                top = jnp.maximum(top, found[:, part * lanes : (part + 1) * lanes])
            top_buf[...] = top
            return inner

        lax.fori_loop(0, count, score, 0)
        highest = jnp.max(top_buf[...], axis=1, keepdims=True) * score_scale
        top_buf[...] = jnp.broadcast_to(highest, top_buf.shape)
        sum_buf[...] = jnp.zeros(sum_buf.shape, jnp.float32)

        def weigh(at, inner):
            top = top_buf[...]
            weights = jnp.concatenate(
                [
                    jnp.exp2(
                        score_buf[at, :, part * lanes : (part + 1) * lanes] * score_scale - top
                    ).astype(jnp.bfloat16)
                    for part in range(rows // lanes)
                ],
                axis=1,
            )
            sum_buf[...] += jnp.dot(
                weights, value_buf[span(at), :], preferred_element_type=jnp.float32
            )
            return inner

        lax.fori_loop(0, count, weigh, 0)
        done_buf[block] = (sum_buf[:, :size] / sum_buf[:, size:]).astype(jnp.bfloat16)

        @pl.when(block != me)
        def _():
            back(block).start()

        @pl.when(block == me)
        def _():
            own_back.start()

        return carry

    lax.fori_loop(0, n, one_block, 0)

    def finish(step, carry):
        peer = lax.rem(me + step, n)
        for copy in outgoing(peer):
            copy.wait_send()
        back(peer).wait_send()
        back_in(peer).wait_recv()
        return carry

    lax.fori_loop(1, n, finish, 0)
    own_back.wait()


def attend_heads(qkv, clip_rows, bias, n):
    _, heads, rows, size = qkv.shape
    lanes = clip_rows.shape[1]
    bf16, f32 = jnp.bfloat16, jnp.float32
    return pl.pallas_call(
        functools.partial(attend_kernel, n, math.log2(math.e) / math.sqrt(size)),
        out_shape=jax.ShapeDtypeStruct((heads, rows, size), bf16),
        in_specs=[
            pl.BlockSpec(memory_space=pltpu.VMEM),
            pl.BlockSpec(memory_space=pltpu.VMEM),
            pl.BlockSpec(memory_space=pltpu.VMEM),
        ],
        out_specs=pl.BlockSpec(memory_space=pltpu.VMEM),
        scratch_shapes=[
            pltpu.VMEM((n * rows, size + lanes), bf16),
            pltpu.VMEM((n * rows, size + lanes), bf16),
            pltpu.VMEM((n * rows, 2 * size), bf16),
            pltpu.VMEM((n, 8, lanes), jnp.int32),
            pltpu.VMEM((n, rows, rows), f32),
            pltpu.VMEM((rows, lanes), f32),
            pltpu.VMEM((rows, 2 * size), f32),
            pltpu.VMEM((n, rows, size), bf16),
            pltpu.SemaphoreType.DMA((4, n)),
            pltpu.SemaphoreType.DMA((4, n)),
            pltpu.SemaphoreType.DMA((4,)),
            pltpu.SemaphoreType.DMA((n,)),
            pltpu.SemaphoreType.DMA((n,)),
            pltpu.SemaphoreType.DMA,
        ],
        compiler_params=pltpu.CompilerParams(
            collective_id=0, has_side_effects=True, vmem_limit_bytes=48 * 2**20
        ),
        cost_estimate=pl.CostEstimate(
            flops=5 * n * n * rows * rows * size, bytes_accessed=4 * n * rows * size * 2,
            transcendentals=n * n * rows * rows // 2,
        ),
    )(qkv, clip_rows, bias)


def project_kernel(
    pieces, attended_ref, weight_ref, out_ref,
    part_buf, send_buf, up_buf, down_buf, send_sem, up_sem, down_sem,
):
    plane = lax.axis_index("head")
    last = part_buf.shape[0] - 1
    rows = part_buf.shape[1]
    width = part_buf.shape[2] // pieces
    heads, size, _ = weight_ref.shape
    middle = (plane > 0) & (plane < last)

    def columns(piece):
        return pl.ds(pl.multiple_of(piece * width, width), width)

    barrier = pltpu.get_barrier_semaphore()

    @pl.when(plane > 0)
    def _():
        pl.semaphore_signal(
            barrier, inc=1, device_id={"head": plane - 1}, device_id_type=pl.DeviceIdType.MESH
        )

    @pl.when(plane < last)
    def _():
        pl.semaphore_signal(
            barrier, inc=1, device_id={"head": plane + 1}, device_id_type=pl.DeviceIdType.MESH
        )

    @pl.when(middle)
    def _():
        pl.semaphore_wait(barrier, 2)

    @pl.when(jnp.logical_not(middle))
    def _():
        pl.semaphore_wait(barrier, 1)

    def upward(share, piece, peer):
        return pltpu.make_async_remote_copy(
            src_ref=send_buf.at[share, :, columns(piece)],
            dst_ref=up_buf.at[share, :, columns(piece)],
            send_sem=send_sem.at[share, piece],
            recv_sem=up_sem.at[share, piece],
            device_id={"head": peer},
            device_id_type=pl.DeviceIdType.MESH,
        )

    def downward(share, piece, peer):
        return pltpu.make_async_remote_copy(
            src_ref=send_buf.at[share, :, columns(piece)],
            dst_ref=down_buf.at[share, :, columns(piece)],
            send_sem=send_sem.at[share, piece],
            recv_sem=down_sem.at[share, piece],
            device_id={"head": peer},
            device_id_type=pl.DeviceIdType.MESH,
        )

    near = jnp.where(plane == 0, 1, plane - 1)
    low = jnp.minimum(plane, last - plane)

    def compute(step, carry):
        order, piece = step // pieces, lax.rem(step, pieces)
        ahead = last - low
        mirrored = jnp.where(order < ahead, last - order, order - ahead)
        share = jnp.where(plane + plane < last, mirrored, last - mirrored)
        at = pl.ds(pl.multiple_of(share * rows, rows), rows)
        left = jnp.concatenate([attended_ref[head, at, :] for head in range(heads)], axis=1)
        right = weight_ref[:, :, columns(piece)].reshape(heads * size, width)
        part = jnp.dot(left, right, preferred_element_type=jnp.float32)
        part_buf[share, :, columns(piece)] = part

        @pl.when((plane == 0) & (share > 0))
        def _():
            send_buf[share, :, columns(piece)] = part.astype(jnp.bfloat16)
            upward(share, piece, plane + 1).start()

        @pl.when((plane == last) & (share < last))
        def _():
            send_buf[share, :, columns(piece)] = part.astype(jnp.bfloat16)
            downward(share, piece, plane - 1).start()

        return carry

    lax.fori_loop(0, (last + 1) * pieces, compute, 0)

    def relay_up(share, piece):
        upward(share, piece, near).wait_recv()
        total = part_buf[share, :, columns(piece)] + up_buf[share, :, columns(piece)].astype(
            jnp.float32
        )
        send_buf[share, :, columns(piece)] = total.astype(jnp.bfloat16)
        upward(share, piece, plane + 1).start()

    def relay_down(share, piece):
        downward(share, piece, near).wait_recv()
        total = part_buf[share, :, columns(piece)] + down_buf[share, :, columns(piece)].astype(
            jnp.float32
        )
        send_buf[share, :, columns(piece)] = total.astype(jnp.bfloat16)
        downward(share, piece, plane - 1).start()

    @pl.when(middle)
    def _():
        def relay(step, carry):
            order, piece = step // pieces, lax.rem(step, pieces)

            @pl.when(order < last - plane)
            def _():
                relay_up(last - order, piece)

            @pl.when(order < plane)
            def _():
                relay_down(order, piece)

            return carry

        lax.fori_loop(0, (last - 1) * pieces, relay, 0)

    def settle(piece, carry):
        part_now = part_buf[plane, :, columns(piece)]

        @pl.when(plane == 0)
        def _():
            downward(plane, piece, near).wait_recv()
            total = part_now + down_buf[plane, :, columns(piece)].astype(jnp.float32)
            out_ref[:, columns(piece)] = total.astype(jnp.bfloat16)

        @pl.when(plane == last)
        def _():
            upward(plane, piece, near).wait_recv()
            total = part_now + up_buf[plane, :, columns(piece)].astype(jnp.float32)
            out_ref[:, columns(piece)] = total.astype(jnp.bfloat16)

        @pl.when(middle)
        def _():
            upward(plane, piece, near).wait_recv()
            downward(plane, piece, near).wait_recv()
            total = (
                part_now
                + up_buf[plane, :, columns(piece)].astype(jnp.float32)
                + down_buf[plane, :, columns(piece)].astype(jnp.float32)
            )
            out_ref[:, columns(piece)] = total.astype(jnp.bfloat16)

        return carry

    lax.fori_loop(0, pieces, settle, 0)

    def finish(step, carry):
        share, piece = step // pieces, lax.rem(step, pieces)

        @pl.when(share != plane)
        def _():
            upward(share, piece, near).wait_send()

        return carry

    lax.fori_loop(0, (last + 1) * pieces, finish, 0)


def project_heads(attended, out_weight, planes):
    heads, rows, size = attended.shape
    model = out_weight.shape[2]
    share = rows // planes
    pieces = 4
    bf16 = jnp.bfloat16
    return pl.pallas_call(
        functools.partial(project_kernel, pieces),
        out_shape=jax.ShapeDtypeStruct((share, model), bf16),
        in_specs=[pl.BlockSpec(memory_space=pltpu.VMEM)] * 2,
        out_specs=pl.BlockSpec(memory_space=pltpu.VMEM),
        scratch_shapes=[
            pltpu.VMEM((planes, share, model), jnp.float32),
            pltpu.VMEM((planes, share, model), bf16),
            pltpu.VMEM((planes, share, model), bf16),
            pltpu.VMEM((planes, share, model), bf16),
            pltpu.SemaphoreType.DMA((planes, pieces)),
            pltpu.SemaphoreType.DMA((planes, pieces)),
            pltpu.SemaphoreType.DMA((planes, pieces)),
        ],
        compiler_params=pltpu.CompilerParams(
            collective_id=1, has_side_effects=True, vmem_limit_bytes=48 * 2**20
        ),
        cost_estimate=pl.CostEstimate(
            flops=2 * rows * heads * size * model,
            bytes_accessed=2 * heads * size * (model + rows),
            transcendentals=0,
        ),
    )(attended, out_weight)


def modulate(activations, mod_table, clip_level, clip_of, clip_count):
    level_count = mod_table.shape[0]
    clip_ids = lax.broadcasted_iota(jnp.int32, (1, clip_count), 1)
    level_ids = lax.broadcasted_iota(jnp.int32, (1, level_count), 1)
    tok_hot = clip_of[:, None] == clip_ids
    level_rows = jnp.sum(jnp.where(tok_hot, clip_level[None, :], 0), axis=1)
    level_hot = (level_rows[:, None] == level_ids).astype(jnp.float32)
    modulation = jnp.dot(level_hot, mod_table, precision=lax.Precision.HIGHEST)
    return (activations.astype(jnp.float32) * (1.0 + modulation)).astype(jnp.bfloat16)


def per_device_heads(
    n, planes, activations, qkv_weight, out_weight, mod_table, clip_level, clip_of, visible
):
    clip_count = visible.shape[0]
    lanes = 128
    moduled = modulate(activations, mod_table, clip_level, clip_of, clip_count)
    qkv = jnp.einsum(
        "td,dchk->chtk", moduled, qkv_weight, preferred_element_type=jnp.float32
    ).astype(jnp.bfloat16)
    clip_rows = clip_of.reshape(-1, lanes)
    clip_rows = jnp.pad(clip_rows, ((0, 8 - clip_rows.shape[0]), (0, 0)))
    bias = jnp.where(visible > 0, 0.0, -(2.0**100)).astype(jnp.bfloat16)
    bias = jnp.pad(bias, ((0, lanes - clip_count), (0, lanes - clip_count)))
    attended = attend_heads(qkv, clip_rows, bias, n)
    return project_heads(attended, out_weight, planes)


def solution(mesh):
    placed = (
        P("ctx", None),
        P(None, None, "head", None),
        P("head", None, None),
        P(),
        P(),
        P("ctx"),
        P(),
    )
    n, planes = mesh.shape["ctx"], mesh.shape["head"]

    def pick(activations, qkv_weight, out_weight, mod_table, clip_level, clip_of, visible):
        rows, heads, size = clip_of.shape[0], qkv_weight.shape[2], qkv_weight.shape[3]
        fits = heads == n and size == 128 and rows % 128 == 0 and 256 <= rows <= 1024
        fits = fits and visible.shape[0] <= 128 and planes == 4
        fits = fits and out_weight.shape[2] % 1024 == 0
        body = functools.partial(per_device_heads, n, planes) if fits else per_device
        return body(activations, qkv_weight, out_weight, mod_table, clip_level, clip_of, visible)

    return jax.shard_map(
        pick, mesh=mesh, in_specs=placed, out_specs=P(("ctx", "head"), None), check_vma=False
    )
```
